32 devices in a mesh: groups: 2 (over y), dp: 4 (over x, core), query: 4 (over z).
Axes of the slice: x: 2, y: 2, z: 4, core: 2. Of those that a mesh axis runs over, the one named last changes fastest.
Arguments:
- hidden: bfloat16 [8192, 14336], P(('groups', 'dp', 'query')), parts along dimension 0, may hold values from -6 to 6
- out_grad: bfloat16 [8192, 4096], P(('groups', 'dp', 'query')), parts along dimension 0, may hold values from -6 to 6
- doc_ids: int32 [8192], P(('groups', 'dp', 'query')), parts along dimension 0, may hold values from 0 to 255, as said below
- proj_in: bfloat16 [64, 14336], replicated, may hold values from -0.046875 to 0.046875
- proj_out: bfloat16 [64, 4096], replicated, may hold values from -0.09375 to 0.09375
- query_grads: bfloat16 [384, 4096], P(('dp', 'query')), may hold values from -0.0234375 to 0.0234375
Outputs:
- scores: float32 [384, 512], P(('dp', 'query'), 'groups'), parts along dimension 1
The draws below stay inside these ranges and needn't reach their ends.
There are 2 independent parts, one for each index of `groups`. The reference program is written for one: setup_inputs(seed, part) draws one part's arguments, and reference() takes and returns one part's arrays. A program takes and returns all parts, laid end to end along the dimension named above; an argument that names none is the same for every part. Nothing has to cross between parts.
Inputs may be any that keep to these rules, and one draw needn't show every extreme that they name: `doc_ids`: never falling along the tokens. The tokens of each device (aligned blocks of 256) hold the last tokens of exactly 16 documents; the first token starts document 0 and the last token ends document 256 - 1.
All inputs are finite; a program needn't handle non-finite values.
Results may differ from the reference program's by a relative error of at most 0.005.
Values may be sent and summed in bfloat16 or wider, within the bound.
A program may use at most 128 MiB of HBM per device.

```python
import jax
import jax.numpy as jnp
from jax import lax

D = 4096
FF = 14336
RANK = 64
TOK_DEV = 256
DOC_DEV = 16
TOKENS = 4096
DOCS = 256
QUERIES = 384


def draw_doc_ids(key, part):
    key = jax.random.fold_in(key, 11)
    blocks = TOKENS // TOK_DEV
    block_keys = jax.random.split(key, blocks)
    orders = jax.vmap(lambda one_key: jax.random.permutation(one_key, TOK_DEV))(block_keys)
    closing = (orders < DOC_DEV).astype(jnp.int32)
    last_order = jax.random.permutation(jax.random.fold_in(key, 5), TOK_DEV - 1)
    last_closing = jnp.concatenate([(last_order < DOC_DEV - 1).astype(jnp.int32), jnp.ones((1,), jnp.int32)])
    row_index = jnp.arange(blocks, dtype=jnp.int32)[:, None]
    closing = jnp.where(row_index == blocks - 1, last_closing[None, :], closing)
    flat = closing.reshape(-1)
    return (jnp.cumsum(flat) - flat).astype(jnp.int32)


def block_levels(own_key, extent, shards, least, largest):
    gain, own = 1.0, jax.random.fold_in(own_key, 6)
    for axis_at, blocks in shards:
        steps = jnp.exp(jax.random.uniform(jax.random.fold_in(own, axis_at), (blocks,), jnp.float32, least / len(shards), largest / len(shards)))
        gain = gain * jnp.repeat(steps, extent[axis_at] // blocks).reshape([-1 if axis == axis_at else 1 for axis in range(len(extent))])
    return gain


def bell_draw(own_key, dims, deviation, most, cuts=(), kind=jnp.bfloat16):
    result = deviation * jax.random.normal(own_key, dims, jnp.float32)
    if cuts:
        result = result * block_levels(own_key, dims, cuts, -0.22, 0.18)
    return jnp.clip(result, -most, most).astype(kind)


def setup_inputs(seed: int = 0, part: int = 0) -> dict:
    splits = jax.random.split(jax.random.key(seed), 7)
    own_keys = jax.random.split(jax.random.fold_in(splits[6], part), 7)
    hidden = bell_draw(own_keys[0], (TOKENS, FF), 1.0, 6.0, ((0, 16),))
    out_grad = bell_draw(own_keys[1], (TOKENS, D), 1.0, 6.0, ((0, 16),))
    doc_ids = draw_doc_ids(jax.random.fold_in(jax.random.fold_in(splits[6], part), 71), part)
    proj_in = bell_draw(splits[3], (RANK, FF), FF ** -0.5, 0.046875)
    proj_out = bell_draw(splits[4], (RANK, D), D ** -0.5, 0.09375)
    query_grads = bell_draw(splits[5], (QUERIES, RANK * RANK), (RANK * RANK * TOK_DEV // DOC_DEV) ** -0.5, 0.0234375, ((0, 16),))
    return {"hidden": hidden, "out_grad": out_grad, "doc_ids": doc_ids, "proj_in": proj_in, "proj_out": proj_out, "query_grads": query_grads}


def reference(hidden, out_grad, doc_ids, proj_in, proj_out, query_grads):
    contract = (((1,), (1,)), ((), ()))
    in_factor = lax.dot_general(hidden, proj_in, contract, preferred_element_type=jnp.float32).astype(jnp.bfloat16)
    out_factor = lax.dot_general(out_grad, proj_out, contract, preferred_element_type=jnp.float32).astype(jnp.bfloat16)
    products = out_factor.astype(jnp.float32)[:, :, None] * in_factor.astype(jnp.float32)[:, None, :]
    products = products.reshape(out_factor.shape[0], RANK * RANK)
    doc_grads = jax.ops.segment_sum(products, doc_ids, num_segments=DOCS).astype(jnp.bfloat16)
    return lax.dot_general(query_grads, doc_grads, contract, preferred_element_type=jnp.float32)
```

```python
import functools

import jax
import jax.numpy as jnp
from jax import lax
from jax.experimental import pallas as pl
from jax.experimental.pallas import tpu as pltpu
from jax.sharding import PartitionSpec as P

DOC_DEV = 16
CHUNK = 2048
NT = (((1,), (1,)), ((), ()))
MESH = pl.DeviceIdType.MESH


def dot_nt(a, b):
    return lax.dot_general(a, b, NT, preferred_element_type=jnp.float32)


def kernel(nd, nq, hid, og, ids, pin, pout, q, out,
           hbuf, obuf, pibuf, pobuf, qin, qall, ofb, ifb, gd, sbuf, rbuf,
           hsem, osem, wsem, qs, qr, os_, or_, is_, ir, ss, sr):
    gi, di, qi = lax.axis_index("groups"), lax.axis_index("dp"), lax.axis_index("query")
    rank, tok = ofb.shape[1] - 16, ofb.shape[2]
    rows_q = q.shape[0]
    nh, no = hid.shape[1] // CHUNK, og.shape[1] // CHUNK

    def dp_peer(p):
        return (gi, lax.rem(di + p, nd), qi)

    def query_peer(p):
        return (gi, di, lax.rem(qi + p, nq))

    q_copy = pltpu.make_async_copy(q, qin, wsem.at[0])
    pout_copy = pltpu.make_async_copy(pout, pobuf, wsem.at[1])
    pin_copy = pltpu.make_async_copy(pin, pibuf, wsem.at[2])
    o_copies = [
        pltpu.make_async_copy(og.at[:, pl.ds(c * CHUNK, CHUNK)], obuf.at[:, pl.ds(c * CHUNK, CHUNK)], osem.at[c])
        for c in range(no)
    ]
    h_copies = [
        pltpu.make_async_copy(hid.at[:, pl.ds(c * CHUNK, CHUNK)], hbuf.at[:, pl.ds(c * CHUNK, CHUNK)], hsem.at[c])
        for c in range(nh)
    ]
    q_copy.start()
    pout_copy.start()
    for copy in o_copies:
        copy.start()
    pin_copy.start()
    for copy in h_copies:
        copy.start()

    barrier = pltpu.get_barrier_semaphore()
    for p in range(1, nd):
        pl.semaphore_signal(barrier, inc=1, device_id=dp_peer(p), device_id_type=MESH)
    for p in range(1, nq):
        pl.semaphore_signal(barrier, inc=1, device_id=query_peer(p), device_id_type=MESH)
    pl.semaphore_wait(barrier, nd + nq - 2)

    q_copy.wait()
    half = q.shape[1] // 2
    qv = qin[...].astype(jnp.float32)
    qall[0] = jnp.concatenate([qv[:, :half], qv[:, half:]], axis=0).astype(jnp.bfloat16)

    def remote(src, dst, send, recv, to):
        return pltpu.make_async_remote_copy(
            src_ref=src, dst_ref=dst, send_sem=send, recv_sem=recv, device_id=to, device_id_type=MESH
        )

    q_sends = [remote(qall.at[0], qall.at[p], qs.at[p], qr.at[p], dp_peer(p)) for p in range(1, nd)]
    for copy in q_sends:
        copy.start()

    gd[...] = jnp.zeros_like(gd)
    pout_copy.wait()
    acc = jnp.zeros((rank, tok), jnp.float32)
    for c in range(no):
        o_copies[c].wait()
        cols = pl.ds(c * CHUNK, CHUNK)
        acc += dot_nt(pobuf[:, cols], obuf[:, cols])
    ofb[0, :rank, :] = acc.astype(jnp.bfloat16)
    slot = (ids[...] - (di * nq + qi) * DOC_DEV).astype(jnp.float32)
    ofb[0, rank:, :] = jnp.broadcast_to(slot, (16, tok)).astype(jnp.bfloat16)
    o_sends = [remote(ofb.at[0], ofb.at[p], os_.at[p], or_.at[p], query_peer(p)) for p in range(1, nq)]
    for copy in o_sends:
        copy.start()

    pin_copy.wait()
    acc = jnp.zeros((rank, tok), jnp.float32)
    for c in range(nh):
        h_copies[c].wait()
        cols = pl.ds(c * CHUNK, CHUNK)
        acc += dot_nt(pibuf[:, cols], hbuf[:, cols])
    ifb[0] = acc.astype(jnp.bfloat16)
    i_sends = [remote(ifb.at[0], ifb.at[p], is_.at[p], ir.at[p], query_peer(p)) for p in range(1, nq)]
    for copy in i_sends:
        copy.start()

    eight = (
        lax.broadcasted_iota(jnp.int32, (8 * rank, rank), 0) // 8
        == lax.broadcasted_iota(jnp.int32, (8 * rank, rank), 1)
    ).astype(jnp.float32).astype(jnp.bfloat16)
    low = lax.broadcasted_iota(jnp.int32, (rank // 2, 8, 2 * rank), 2) < rank
    sub = lax.broadcasted_iota(jnp.int32, (8, tok), 0).astype(jnp.float32)
    width = 2 * rank
    for p in range(nq):
        if p:
            o_sends[p - 1].wait_recv()
        of = ofb[p, :rank, :]
        doc = ofb[p, rank:, :].astype(jnp.float32)[:8]
        in_0, in_2 = doc < 8, doc >= 16
        in_1 = jnp.logical_not(jnp.logical_or(in_0, in_2))
        base = jnp.where(in_0, 0.0, jnp.where(in_2, 16.0, 8.0))
        mine = (doc - base == sub).astype(jnp.float32)
        rep = jnp.dot(eight, of, preferred_element_type=jnp.float32)
        a = (rep.reshape(rank, 8, tok) * mine[None]).reshape(8 * rank, tok).astype(jnp.bfloat16)
        if p:
            i_sends[p - 1].wait_recv()
        inf = ifb[p].astype(jnp.float32)
        b0, b1, b2 = (
            jnp.where(jnp.broadcast_to(m[:1], inf.shape), inf, 0.0).astype(jnp.bfloat16) for m in (in_0, in_1, in_2)
        )
        g = dot_nt(a, jnp.concatenate([b0, b1, b1, b0, b2, b2], axis=0))
        g = g.reshape(rank // 2, 16, 3 * width)
        even, odd = g[:, :8, :], g[:, 8:, :]
        g0 = jnp.where(low, even[:, :, :width], odd[:, :, width:2 * width])
        g1 = jnp.where(low, even[:, :, width:2 * width], odd[:, :, :width])
        g2 = jnp.where(low, even[:, :, 2 * width:], odd[:, :, 2 * width:])
        row = pl.multiple_of(lax.rem(qi + nq - p, nq) * DOC_DEV, DOC_DEV)
        gd[:, pl.ds(row, 8), :] += g0
        gd[:, pl.ds(row + 8, 8), :] = g1
        gd[:, pl.ds(row + 16, 8), :] += g2

    for copy in q_sends:
        copy.wait_recv()
    queries = qall[...].reshape(nd * 2 * rows_q, half)
    pairs = rank // 4
    total = []
    for h in range(2):
        docs = jnp.concatenate([gd[h * pairs + m] for m in range(pairs)], axis=1).astype(jnp.bfloat16)
        total.append(dot_nt(queries, docs))
    for p in range(nd):
        at = 2 * p * rows_q
        sbuf[p] = total[0][at:at + rows_q] + total[1][at + rows_q:at + 2 * rows_q]
    s_sends = [remote(sbuf.at[p], rbuf.at[p], ss.at[p], sr.at[p], dp_peer(nd - p)) for p in range(1, nd)]
    for copy in s_sends:
        copy.start()
    rbuf[0] = sbuf[0]
    for copy in s_sends:
        copy.wait_recv()

    per_row = nq * DOC_DEV
    got = [rbuf[lax.rem(r + nd - di, nd)] for r in range(nd)]
    if per_row % 128 == 0:
        for r in range(nd):
            value = got[r][:, :per_row]
            if r:
                value = value + jnp.pad(got[r - 1][:, per_row:per_row + 128], ((0, 0), (0, per_row - 128)))
            out[:, r * per_row:(r + 1) * per_row] = value
    else:
        left = lax.broadcasted_iota(jnp.int32, got[0].shape, 1) < 64
        turned = [pltpu.roll(got[r], 64, 1) if r % 2 else None for r in range(nd)]
        for m in range(nd // 2):
            value = got[2 * m] + jnp.where(left, 0.0, turned[2 * m + 1])
            if m:
                value = value + jnp.where(left, turned[2 * m - 1], 0.0)
            out[:, m * 128:(m + 1) * 128] = value
    for copy in q_sends + o_sends + i_sends + s_sends:
        copy.wait_send()


def solution(mesh):
    nd, nq = mesh.shape["dp"], mesh.shape["query"]

    def on_device(hidden, out_grad, doc_ids, proj_in, proj_out, query_grads):
        tok, ff = hidden.shape
        d = out_grad.shape[1]
        rank = proj_in.shape[0]
        rows_q, flat = query_grads.shape
        per_row = nq * DOC_DEV
        assert rank == 64 and flat == rank * rank and (per_row == 64 or per_row % 128 == 0)
        docs = -(-(per_row + 16) // 128) * 128
        bf16, f32 = jnp.bfloat16, jnp.float32
        dma = pltpu.SemaphoreType.DMA
        hbm = pl.BlockSpec(memory_space=pl.ANY)
        vmem = pl.BlockSpec(memory_space=pltpu.VMEM)
        return pl.pallas_call(
            functools.partial(kernel, nd, nq),
            out_shape=jax.ShapeDtypeStruct((rows_q, nd * per_row), f32),
            in_specs=[hbm, hbm, vmem, hbm, hbm, hbm],
            out_specs=vmem,
            scratch_shapes=[
                pltpu.VMEM((tok, ff), bf16),
                pltpu.VMEM((tok, d), bf16),
                pltpu.VMEM((rank, ff), bf16),
                pltpu.VMEM((rank, d), bf16),
                pltpu.VMEM((rows_q, flat), bf16),
                pltpu.VMEM((nd, 2 * rows_q, flat // 2), bf16),
                pltpu.VMEM((nq, rank + 16, tok), bf16),
                pltpu.VMEM((nq, rank, tok), bf16),
                pltpu.VMEM((rank // 2, docs, 2 * rank), f32),
                pltpu.VMEM((nd, rows_q, docs), f32),
                pltpu.VMEM((nd, rows_q, docs), f32),
                dma((ff // CHUNK,)),
                dma((d // CHUNK,)),
                dma((3,)),
                dma((nd,)),
                dma((nd,)),
                dma((nq,)),
                dma((nq,)),
                dma((nq,)),
                dma((nq,)),
                dma((nd,)),
                dma((nd,)),
            ],
            compiler_params=pltpu.CompilerParams(
                collective_id=0, has_side_effects=True, vmem_limit_bytes=48 * 1024 * 1024
            ),
        )(hidden, out_grad, doc_ids.reshape(1, tok), proj_in, proj_out, query_grads)

    placed = (
        P(("groups", "dp", "query"), None),
        P(("groups", "dp", "query"), None),
        P(("groups", "dp", "query")),
        P(),
        P(),
        P(("dp", "query"), None),
    )
    return jax.shard_map(
        on_device, mesh=mesh, in_specs=placed, out_specs=P(("dp", "query"), "groups"), check_vma=False
    )
```

```python
import functools

import jax
import jax.numpy as jnp
from jax import lax
from jax.experimental import pallas as pl
from jax.experimental.pallas import tpu as pltpu
from jax.sharding import PartitionSpec as P

DOC_DEV = 16
CHUNK = 2048
NT = (((1,), (1,)), ((), ()))
MESH = pl.DeviceIdType.MESH


def dot_nt(a, b):
    return lax.dot_general(a, b, NT, preferred_element_type=jnp.float32)


def kernel(nd, nq, hid, og, ids, pin, pout, q, out,
           hbuf, obuf, pibuf, pobuf, idbuf, qin, qall, ofb, ifb, gd, sbuf, rbuf,
           hsem, osem, wsem, qs, qr, os_, or_, is_, ir, ss, sr):
    gi, di, qi = lax.axis_index("groups"), lax.axis_index("dp"), lax.axis_index("query")
    rank, tok = ofb.shape[1] - 16, ofb.shape[2]
    rows_q = q.shape[0]
    nh, no = hid.shape[1] // CHUNK, og.shape[1] // CHUNK

    def dp_peer(p):
        return (gi, lax.rem(di + p, nd), qi)

    def query_peer(p):
        return (gi, di, lax.rem(qi + p, nq))

    q_copy = pltpu.make_async_copy(q, qin, wsem.at[0])
    pout_copy = pltpu.make_async_copy(pout, pobuf, wsem.at[1])
    pin_copy = pltpu.make_async_copy(pin, pibuf, wsem.at[2])
    o_copies = [
        pltpu.make_async_copy(og.at[:, pl.ds(c * CHUNK, CHUNK)], obuf.at[:, pl.ds(c * CHUNK, CHUNK)], osem.at[c])
        for c in range(no)
    ]
    h_copies = [
        pltpu.make_async_copy(hid.at[:, pl.ds(c * CHUNK, CHUNK)], hbuf.at[:, pl.ds(c * CHUNK, CHUNK)], hsem.at[c])
        for c in range(nh)
    ]
    id_copy = pltpu.make_async_copy(ids, idbuf, wsem.at[3])
    q_copy.start()
    id_copy.start()
    pout_copy.start()
    for copy in o_copies:
        copy.start()
    pin_copy.start()
    for copy in h_copies:
        copy.start()

    barrier = pltpu.get_barrier_semaphore()
    for p in range(1, nd):
        pl.semaphore_signal(barrier, inc=1, device_id=dp_peer(p), device_id_type=MESH)
    for p in range(1, nq):
        pl.semaphore_signal(barrier, inc=1, device_id=query_peer(p), device_id_type=MESH)
    pl.semaphore_wait(barrier, nd + nq - 2)

    q_copy.wait()
    half = q.shape[1] // 2
    qv = qin[...].astype(jnp.float32)
    qall[0] = jnp.concatenate([qv[:, :half], qv[:, half:]], axis=0).astype(jnp.bfloat16)

    def remote(src, dst, send, recv, to):
        return pltpu.make_async_remote_copy(
            src_ref=src, dst_ref=dst, send_sem=send, recv_sem=recv, device_id=to, device_id_type=MESH
        )

    q_sends = [remote(qall.at[0], qall.at[p], qs.at[p], qr.at[p], dp_peer(p)) for p in range(1, nd)]
    for copy in q_sends:
        copy.start()

    gd[...] = jnp.zeros_like(gd)
    pout_copy.wait()
    acc = jnp.zeros((rank, tok), jnp.float32)
    for c in range(no):
        o_copies[c].wait()
        cols = pl.ds(c * CHUNK, CHUNK)
        acc += dot_nt(pobuf[:, cols], obuf[:, cols])
    ofb[0, :rank, :] = acc.astype(jnp.bfloat16)
    id_copy.wait()
    slot = (idbuf[...] - (di * nq + qi) * DOC_DEV).astype(jnp.float32)
    ofb[0, rank:, :] = jnp.broadcast_to(slot, (16, tok)).astype(jnp.bfloat16)
    o_sends = [remote(ofb.at[0], ofb.at[p], os_.at[p], or_.at[p], query_peer(p)) for p in range(1, nq)]
    for copy in o_sends:
        copy.start()

    pin_copy.wait()
    acc = jnp.zeros((rank, tok), jnp.float32)
    for c in range(nh):
        h_copies[c].wait()
        cols = pl.ds(c * CHUNK, CHUNK)
        acc += dot_nt(pibuf[:, cols], hbuf[:, cols])
    ifb[0] = acc.astype(jnp.bfloat16)
    i_sends = [remote(ifb.at[0], ifb.at[p], is_.at[p], ir.at[p], query_peer(p)) for p in range(1, nq)]
    for copy in i_sends:
        copy.start()

    eight = (
        lax.broadcasted_iota(jnp.int32, (8 * rank, rank), 0) // 8
        == lax.broadcasted_iota(jnp.int32, (8 * rank, rank), 1)
    ).astype(jnp.float32).astype(jnp.bfloat16)
    low = lax.broadcasted_iota(jnp.int32, (rank // 2, 8, 2 * rank), 2) < rank
    sub = lax.broadcasted_iota(jnp.int32, (8, tok), 0).astype(jnp.float32)
    width = 2 * rank
    for p in range(nq):
        if p:
            o_sends[p - 1].wait_recv()
        of = ofb[p, :rank, :]
        doc = ofb[p, rank:, :].astype(jnp.float32)[:8]
        in_0, in_2 = doc < 8, doc >= 16
        in_1 = jnp.logical_not(jnp.logical_or(in_0, in_2))
        base = jnp.where(in_0, 0.0, jnp.where(in_2, 16.0, 8.0))
        mine = (doc - base == sub).astype(jnp.float32)
        rep = jnp.dot(eight, of, preferred_element_type=jnp.float32)
        a = (rep.reshape(rank, 8, tok) * mine[None]).reshape(8 * rank, tok).astype(jnp.bfloat16)
        if p:
            i_sends[p - 1].wait_recv()
        inf = ifb[p].astype(jnp.float32)
        b0, b1, b2 = (
            jnp.where(jnp.broadcast_to(m[:1], inf.shape), inf, 0.0).astype(jnp.bfloat16) for m in (in_0, in_1, in_2)
        )
        g = dot_nt(a, jnp.concatenate([b0, b1, b1, b0, b2, b2], axis=0))
        g = g.reshape(rank // 2, 16, 3 * width)
        even, odd = g[:, :8, :], g[:, 8:, :]
        g0 = jnp.where(low, even[:, :, :width], odd[:, :, width:2 * width])
        g1 = jnp.where(low, even[:, :, width:2 * width], odd[:, :, :width])
        g2 = jnp.where(low, even[:, :, 2 * width:], odd[:, :, 2 * width:])
        row = pl.multiple_of(lax.rem(qi + nq - p, nq) * DOC_DEV, DOC_DEV)
        gd[:, pl.ds(row, 8), :] += g0
        gd[:, pl.ds(row + 8, 8), :] = g1
        gd[:, pl.ds(row + 16, 8), :] += g2

    for copy in q_sends:
        copy.wait_recv()
    queries = qall[...].reshape(nd * 2 * rows_q, half)
    pairs = rank // 4
    total = []
    for h in range(2):
        docs = jnp.concatenate([gd[h * pairs + m] for m in range(pairs)], axis=1).astype(jnp.bfloat16)
        total.append(dot_nt(queries, docs))
    for p in range(nd):
        at = 2 * p * rows_q
        sbuf[p] = total[0][at:at + rows_q] + total[1][at + rows_q:at + 2 * rows_q]
    s_sends = [remote(sbuf.at[p], rbuf.at[p], ss.at[p], sr.at[p], dp_peer(nd - p)) for p in range(1, nd)]
    for copy in s_sends:
        copy.start()
    rbuf[0] = sbuf[0]
    for copy in s_sends:
        copy.wait_recv()

    per_row = nq * DOC_DEV
    got = [rbuf[lax.rem(r + nd - di, nd)] for r in range(nd)]
    if per_row % 128 == 0:
        for r in range(nd):
            value = got[r][:, :per_row]
            if r:
                value = value + jnp.pad(got[r - 1][:, per_row:per_row + 128], ((0, 0), (0, per_row - 128)))
            out[:, r * per_row:(r + 1) * per_row] = value
    else:
        left = lax.broadcasted_iota(jnp.int32, got[0].shape, 1) < 64
        turned = [pltpu.roll(got[r], 64, 1) if r % 2 else None for r in range(nd)]
        for m in range(nd // 2):
            value = got[2 * m] + jnp.where(left, 0.0, turned[2 * m + 1])
            if m:
                value = value + jnp.where(left, turned[2 * m - 1], 0.0)
            out[:, m * 128:(m + 1) * 128] = value
    for copy in q_sends + o_sends + i_sends + s_sends:
        copy.wait_send()


def solution(mesh):
    nd, nq = mesh.shape["dp"], mesh.shape["query"]

    def on_device(hidden, out_grad, doc_ids, proj_in, proj_out, query_grads):
        tok, ff = hidden.shape
        d = out_grad.shape[1]
        rank = proj_in.shape[0]
        rows_q, flat = query_grads.shape
        per_row = nq * DOC_DEV
        assert rank == 64 and flat == rank * rank and (per_row == 64 or per_row % 128 == 0)
        docs = -(-(per_row + 16) // 128) * 128
        bf16, f32 = jnp.bfloat16, jnp.float32
        dma = pltpu.SemaphoreType.DMA
        hbm = pl.BlockSpec(memory_space=pltpu.HBM)
        vmem = pl.BlockSpec(memory_space=pltpu.VMEM)
        return pl.pallas_call(
            functools.partial(kernel, nd, nq),
            out_shape=jax.ShapeDtypeStruct((rows_q, nd * per_row), f32),
            in_specs=[hbm] * 6,
            out_specs=vmem,
            scratch_shapes=[
                pltpu.VMEM((tok, ff), bf16),
                pltpu.VMEM((tok, d), bf16),
                pltpu.VMEM((rank, ff), bf16),
                pltpu.VMEM((rank, d), bf16),
                pltpu.VMEM((1, tok), jnp.int32),
                pltpu.VMEM((rows_q, flat), bf16),
                pltpu.VMEM((nd, 2 * rows_q, flat // 2), bf16),
                pltpu.VMEM((nq, rank + 16, tok), bf16),
                pltpu.VMEM((nq, rank, tok), bf16),
                pltpu.VMEM((rank // 2, docs, 2 * rank), f32),
                pltpu.VMEM((nd, rows_q, docs), f32),
                pltpu.VMEM((nd, rows_q, docs), f32),
                dma((ff // CHUNK,)),
                dma((d // CHUNK,)),
                dma((4,)),
                dma((nd,)),
                dma((nd,)),
                dma((nq,)),
                dma((nq,)),
                dma((nq,)),
                dma((nq,)),
                dma((nd,)),
                dma((nd,)),
            ],
            compiler_params=pltpu.CompilerParams(
                collective_id=0, has_side_effects=True, vmem_limit_bytes=60 * 1024 * 1024
            ),
        )(hidden, out_grad, doc_ids.reshape(1, tok), proj_in, proj_out, query_grads)

    placed = (
        P(("groups", "dp", "query"), None),
        P(("groups", "dp", "query"), None),
        P(("groups", "dp", "query")),
        P(),
        P(),
        P(("dp", "query"), None),
    )
    return jax.shard_map(
        on_device, mesh=mesh, in_specs=placed, out_specs=P(("dp", "query"), "groups"), check_vma=False
    )
```

```python
import functools

import jax
import jax.numpy as jnp
from jax import lax
from jax.experimental import pallas as pl
from jax.experimental.pallas import tpu as pltpu
from jax.sharding import PartitionSpec as P

DOC_DEV = 16
STEP = 256
O_WIDTHS = (4, 6, 6)
H_WIDTHS = (8, 8, 10, 14, 16)
NT = (((1,), (1,)), ((), ()))
MESH = pl.DeviceIdType.MESH


def chunks(total, widths):
    units, whole = total // STEP, sum(widths)
    ends = [units * sum(widths[:i + 1]) // whole * STEP for i in range(len(widths))]
    return [(a, b - a) for a, b in zip([0] + ends[:-1], ends)]


def dot_nt(a, b):
    return lax.dot_general(a, b, NT, preferred_element_type=jnp.float32)


def kernel(nd, nq, hid, og, ids, pin, pout, q, out,
           hbuf, obuf, pibuf, pobuf, idbuf, qin, qall, ofb, ifb, amask, gd, sbuf, rbuf,
           hsem, osem, pisem, posem, wsem, qs, qr, os_, or_, is_, ir, ss, sr):
    gi, di, qi = lax.axis_index("groups"), lax.axis_index("dp"), lax.axis_index("query")
    rank, tok = ofb.shape[1] - 16, ofb.shape[2]
    rows_q = q.shape[0]
    o_cols = chunks(og.shape[1], O_WIDTHS)
    h_cols = chunks(hid.shape[1], H_WIDTHS)

    def dp_peer(p):
        return (gi, lax.rem(di + p, nd), qi)

    def query_peer(p):
        return (gi, di, lax.rem(qi + p, nq))

    def by_columns(source, target, columns, sems):
        return [
            pltpu.make_async_copy(source.at[:, pl.ds(at, n)], target.at[:, pl.ds(at, n)], sems.at[c])
            for c, (at, n) in enumerate(columns)
        ]

    po_copies = by_columns(pout, pobuf, o_cols, posem)
    o_copies = by_columns(og, obuf, o_cols, osem)
    pi_copies = by_columns(pin, pibuf, h_cols, pisem)
    h_copies = by_columns(hid, hbuf, h_cols, hsem)
    q_copy = pltpu.make_async_copy(q, qin, wsem.at[0])
    id_copy = pltpu.make_async_copy(ids, idbuf, wsem.at[1])
    q_copy.start()
    id_copy.start()
    for weight, tokens in zip(po_copies + pi_copies, o_copies + h_copies):
        weight.start()
        tokens.start()

    barrier = pltpu.get_barrier_semaphore()
    for p in range(1, nd):
        pl.semaphore_signal(barrier, inc=1, device_id=dp_peer(p), device_id_type=MESH)
    for p in range(1, nq):
        pl.semaphore_signal(barrier, inc=1, device_id=query_peer(p), device_id_type=MESH)
    pl.semaphore_wait(barrier, nd + nq - 2)

    q_copy.wait()
    half = q.shape[1] // 2
    qv = qin[...].astype(jnp.float32)
    qall[0] = jnp.concatenate([qv[:, :half], qv[:, half:]], axis=0).astype(jnp.bfloat16)

    def remote(src, dst, send, recv, to):
        return pltpu.make_async_remote_copy(
            src_ref=src, dst_ref=dst, send_sem=send, recv_sem=recv, device_id=to, device_id_type=MESH
        )

    q_sends = [remote(qall.at[0], qall.at[p], qs.at[p], qr.at[p], dp_peer(p)) for p in range(1, nd)]
    for copy in q_sends:
        copy.start()

    gd[...] = jnp.zeros_like(gd)
    acc = jnp.zeros((rank, tok), jnp.float32)
    for c, (at, n) in enumerate(o_cols):
        po_copies[c].wait()
        o_copies[c].wait()
        cols = pl.ds(at, n)
        acc += dot_nt(pobuf[:, cols], obuf[:, cols])
    ofb[0, :rank, :] = acc.astype(jnp.bfloat16)
    id_copy.wait()
    slot = (idbuf[...] - (di * nq + qi) * DOC_DEV).astype(jnp.float32)
    ofb[0, rank:, :] = jnp.broadcast_to(slot, (16, tok)).astype(jnp.bfloat16)
    o_sends = [remote(ofb.at[0], ofb.at[p], os_.at[p], or_.at[p], query_peer(p)) for p in range(1, nq)]
    for copy in o_sends:
        copy.start()

    eight = (
        lax.broadcasted_iota(jnp.int32, (8 * rank, rank), 0) // 8
        == lax.broadcasted_iota(jnp.int32, (8 * rank, rank), 1)
    ).astype(jnp.float32).astype(jnp.bfloat16)
    sub = lax.broadcasted_iota(jnp.int32, (8, tok), 0).astype(jnp.float32)

    def which(p):
        doc = ofb[p, rank:, :].astype(jnp.float32)[:8]
        first, past = doc < 8, doc >= 16
        return doc, first, jnp.logical_not(jnp.logical_or(first, past)), past

    def spread(p):
        doc, first, _, past = which(p)
        base = jnp.where(first, 0.0, jnp.where(past, 16.0, 8.0))
        mine = (doc - base == sub).astype(jnp.float32)
        rep = jnp.dot(eight, ofb[p, :rank, :], preferred_element_type=jnp.float32)
        amask[p] = (rep.reshape(rank, 8, tok) * mine[None]).reshape(8 * rank, tok).astype(jnp.bfloat16)

    spread(0)

    acc = jnp.zeros((rank, tok), jnp.float32)
    for c, (at, n) in enumerate(h_cols):
        pi_copies[c].wait()
        h_copies[c].wait()
        cols = pl.ds(at, n)
        acc += dot_nt(pibuf[:, cols], hbuf[:, cols])
    ifb[0] = acc.astype(jnp.bfloat16)
    i_sends = [remote(ifb.at[0], ifb.at[p], is_.at[p], ir.at[p], query_peer(p)) for p in range(1, nq)]
    for copy in i_sends:
        copy.start()
    for p in range(1, nq):
        o_sends[p - 1].wait_recv()
        spread(p)

    low = lax.broadcasted_iota(jnp.int32, (rank // 2, 8, 2 * rank), 2) < rank
    width = 2 * rank
    for p in range(nq):
        if p:
            i_sends[p - 1].wait_recv()
        _, in_0, in_1, in_2 = which(p)
        inf = ifb[p].astype(jnp.float32)
        b0, b1, b2 = (
            jnp.where(jnp.broadcast_to(m[:1], inf.shape), inf, 0.0).astype(jnp.bfloat16) for m in (in_0, in_1, in_2)
        )
        g = dot_nt(amask[p], jnp.concatenate([b0, b1, b1, b0, b2, b2], axis=0))
        g = g.reshape(rank // 2, 16, 3 * width)
        even, odd = g[:, :8, :], g[:, 8:, :]
        g0 = jnp.where(low, even[:, :, :width], odd[:, :, width:2 * width])
        g1 = jnp.where(low, even[:, :, width:2 * width], odd[:, :, :width])
        g2 = jnp.where(low, even[:, :, 2 * width:], odd[:, :, 2 * width:])
        row = pl.multiple_of(lax.rem(qi + nq - p, nq) * DOC_DEV, DOC_DEV)
        gd[:, pl.ds(row, 8), :] += g0
        gd[:, pl.ds(row + 8, 8), :] = g1
        gd[:, pl.ds(row + 16, 8), :] += g2

    for copy in q_sends:
        copy.wait_recv()
    queries = qall[...].reshape(nd * 2 * rows_q, half)
    pairs = rank // 4
    total = []
    for h in range(2):
        docs = jnp.concatenate([gd[h * pairs + m] for m in range(pairs)], axis=1).astype(jnp.bfloat16)
        total.append(dot_nt(queries, docs))
    for p in range(nd):
        at = 2 * p * rows_q
        sbuf[p] = total[0][at:at + rows_q] + total[1][at + rows_q:at + 2 * rows_q]
    s_sends = [remote(sbuf.at[p], rbuf.at[p], ss.at[p], sr.at[p], dp_peer(nd - p)) for p in range(1, nd)]
    for copy in s_sends:
        copy.start()
    rbuf[0] = sbuf[0]
    for copy in s_sends:
        copy.wait_recv()

    per_row = nq * DOC_DEV
    got = [rbuf[lax.rem(r + nd - di, nd)] for r in range(nd)]
    if per_row % 128 == 0:
        for r in range(nd):
            value = got[r][:, :per_row]
            if r:
                value = value + jnp.pad(got[r - 1][:, per_row:per_row + 128], ((0, 0), (0, per_row - 128)))
            out[:, r * per_row:(r + 1) * per_row] = value
    else:
        left = lax.broadcasted_iota(jnp.int32, got[0].shape, 1) < 64
        turned = [pltpu.roll(got[r], 64, 1) if r % 2 else None for r in range(nd)]
        for m in range(nd // 2):
            value = got[2 * m] + jnp.where(left, 0.0, turned[2 * m + 1])
            if m:
                value = value + jnp.where(left, turned[2 * m - 1], 0.0)
            out[:, m * 128:(m + 1) * 128] = value
    for copy in q_sends + o_sends + i_sends + s_sends:
        copy.wait_send()


def solution(mesh):
    nd, nq = mesh.shape["dp"], mesh.shape["query"]

    def on_device(hidden, out_grad, doc_ids, proj_in, proj_out, query_grads):
        tok, ff = hidden.shape
        d = out_grad.shape[1]
        rank = proj_in.shape[0]
        rows_q, flat = query_grads.shape
        per_row = nq * DOC_DEV
        assert rank == 64 and flat == rank * rank and (per_row == 64 or per_row % 128 == 0)
        docs = -(-(per_row + 16) // 128) * 128
        bf16, f32 = jnp.bfloat16, jnp.float32
        dma = pltpu.SemaphoreType.DMA
        hbm = pl.BlockSpec(memory_space=pltpu.HBM)
        vmem = pl.BlockSpec(memory_space=pltpu.VMEM)
        return pl.pallas_call(
            functools.partial(kernel, nd, nq),
            out_shape=jax.ShapeDtypeStruct((rows_q, nd * per_row), f32),
            in_specs=[hbm] * 6,
            out_specs=vmem,
            scratch_shapes=[
                pltpu.VMEM((tok, ff), bf16),
                pltpu.VMEM((tok, d), bf16),
                pltpu.VMEM((rank, ff), bf16),
                pltpu.VMEM((rank, d), bf16),
                pltpu.VMEM((1, tok), jnp.int32),
                pltpu.VMEM((rows_q, flat), bf16),
                pltpu.VMEM((nd, 2 * rows_q, flat // 2), bf16),
                pltpu.VMEM((nq, rank + 16, tok), bf16),
                pltpu.VMEM((nq, rank, tok), bf16),
                pltpu.VMEM((nq, 8 * rank, tok), bf16),
                pltpu.VMEM((rank // 2, docs, 2 * rank), f32),
                pltpu.VMEM((nd, rows_q, docs), f32),
                pltpu.VMEM((nd, rows_q, docs), f32),
                dma((len(H_WIDTHS),)),
                dma((len(O_WIDTHS),)),
                dma((len(H_WIDTHS),)),
                dma((len(O_WIDTHS),)),
                dma((2,)),
                dma((nd,)),
                dma((nd,)),
                dma((nq,)),
                dma((nq,)),
                dma((nq,)),
                dma((nq,)),
                dma((nd,)),
                dma((nd,)),
            ],
            compiler_params=pltpu.CompilerParams(
                collective_id=0, has_side_effects=True, vmem_limit_bytes=60 * 1024 * 1024
            ),
        )(hidden, out_grad, doc_ids.reshape(1, tok), proj_in, proj_out, query_grads)

    placed = (
        P(("groups", "dp", "query"), None),
        P(("groups", "dp", "query"), None),
        P(("groups", "dp", "query")),
        P(),
        P(),
        P(("dp", "query"), None),
    )
    return jax.shard_map(
        on_device, mesh=mesh, in_specs=placed, out_specs=P(("dp", "query"), "groups"), check_vma=False
    )
```

```python
import functools

import jax
import jax.numpy as jnp
from jax import lax
from jax.experimental import pallas as pl
from jax.experimental.pallas import tpu as pltpu
from jax.sharding import PartitionSpec as P

DOC_DEV = 16
STEP = 256
O_WIDTHS = (4, 6, 6)
H_WIDTHS = (8, 8, 10, 14, 16)
NT = (((1,), (1,)), ((), ()))
MESH = pl.DeviceIdType.MESH


def chunks(total, widths):
    units, whole = total // STEP, sum(widths)
    ends = [units * sum(widths[:i + 1]) // whole * STEP for i in range(len(widths))]
    return [(a, b - a) for a, b in zip([0] + ends[:-1], ends)]


def dot_nt(a, b):
    return lax.dot_general(a, b, NT, preferred_element_type=jnp.float32)


def kernel(nd, nq, hid, og, ids, pin, pout, q, out,
           hbuf, obuf, pibuf, pobuf, idbuf, qin, qall, ofb, ifb, amask, gd, sbuf, rbuf,
           hsem, osem, pisem, posem, wsem, qs, qr, os_, or_, is_, ir, ss, sr):
    gi, di, qi = lax.axis_index("groups"), lax.axis_index("dp"), lax.axis_index("query")
    rank, tok = ofb.shape[1] - 16, ofb.shape[2]
    rows_q = q.shape[0]
    o_cols = chunks(og.shape[1], O_WIDTHS)
    h_cols = chunks(hid.shape[1], H_WIDTHS)

    def dp_peer(p):
        return (gi, lax.rem(di + p, nd), qi)

    def query_peer(p):
        return (gi, di, lax.rem(qi + p, nq))

    def by_columns(source, target, columns, sems):
        return [
            pltpu.make_async_copy(source.at[:, pl.ds(at, n)], target.at[:, pl.ds(at, n)], sems.at[c])
            for c, (at, n) in enumerate(columns)
        ]

    po_copies = by_columns(pout, pobuf, o_cols, posem)
    o_copies = by_columns(og, obuf, o_cols, osem)
    pi_copies = by_columns(pin, pibuf, h_cols, pisem)
    h_copies = by_columns(hid, hbuf, h_cols, hsem)
    q_copy = pltpu.make_async_copy(q, qin, wsem.at[0])
    id_copy = pltpu.make_async_copy(ids, idbuf, wsem.at[1])
    q_copy.start()
    id_copy.start()
    for weight, tokens in zip(po_copies + pi_copies, o_copies + h_copies):
        weight.start()
        tokens.start()

    barrier = pltpu.get_barrier_semaphore()
    for p in range(1, nd):
        pl.semaphore_signal(barrier, inc=1, device_id=dp_peer(p), device_id_type=MESH)
    for p in range(1, nq):
        pl.semaphore_signal(barrier, inc=1, device_id=query_peer(p), device_id_type=MESH)
    pl.semaphore_wait(barrier, nd + nq - 2)

    q_copy.wait()
    half = q.shape[1] // 2
    qv = qin[...].astype(jnp.float32)
    qall[0] = jnp.concatenate([qv[:, :half], qv[:, half:]], axis=0).astype(jnp.bfloat16)

    def remote(src, dst, send, recv, to):
        return pltpu.make_async_remote_copy(
            src_ref=src, dst_ref=dst, send_sem=send, recv_sem=recv, device_id=to, device_id_type=MESH
        )

    q_sends = [remote(qall.at[0], qall.at[p], qs.at[p], qr.at[p], dp_peer(p)) for p in range(1, nd)]
    for copy in q_sends:
        copy.start()

    acc = jnp.zeros((rank, tok), jnp.float32)
    for c, (at, n) in enumerate(o_cols):
        po_copies[c].wait()
        o_copies[c].wait()
        cols = pl.ds(at, n)
        acc += dot_nt(pobuf[:, cols], obuf[:, cols])
    ofb[0, :rank, :] = acc.astype(jnp.bfloat16)
    id_copy.wait()
    slot = (idbuf[...] - (di * nq + qi) * DOC_DEV).astype(jnp.float32)
    ofb[0, rank:, :] = jnp.broadcast_to(slot, (16, tok)).astype(jnp.bfloat16)
    o_sends = [remote(ofb.at[0], ofb.at[p], os_.at[p], or_.at[p], query_peer(p)) for p in range(1, nq)]
    for copy in o_sends:
        copy.start()

    eight = (
        lax.broadcasted_iota(jnp.int32, (8 * rank, rank), 0) // 8
        == lax.broadcasted_iota(jnp.int32, (8 * rank, rank), 1)
    ).astype(jnp.float32).astype(jnp.bfloat16)
    sub = lax.broadcasted_iota(jnp.int32, (8, tok), 0).astype(jnp.float32)

    def which(p):
        doc = ofb[p, rank:, :].astype(jnp.float32)[:8]
        first, past = doc < 8, doc >= 16
        return doc, first, jnp.logical_not(jnp.logical_or(first, past)), past

    def spread(p):
        doc, first, _, past = which(p)
        base = jnp.where(first, 0.0, jnp.where(past, 16.0, 8.0))
        mine = (doc - base == sub).astype(jnp.float32)
        rep = jnp.dot(eight, ofb[p, :rank, :], preferred_element_type=jnp.float32)
        amask[p] = (rep.reshape(rank, 8, tok) * mine[None]).reshape(8 * rank, tok).astype(jnp.bfloat16)

    spread(0)

    acc = jnp.zeros((rank, tok), jnp.float32)
    for c, (at, n) in enumerate(h_cols):
        pi_copies[c].wait()
        h_copies[c].wait()
        cols = pl.ds(at, n)
        acc += dot_nt(pibuf[:, cols], hbuf[:, cols])
    ifb[0] = acc.astype(jnp.bfloat16)
    i_sends = [remote(ifb.at[0], ifb.at[p], is_.at[p], ir.at[p], query_peer(p)) for p in range(1, nq)]
    for copy in i_sends:
        copy.start()
    for p in range(1, nq):
        o_sends[p - 1].wait_recv()
        spread(p)

    low = lax.broadcasted_iota(jnp.int32, (rank // 2, 8, 2 * rank), 2) < rank
    width = 2 * rank
    for p in range(nq):
        if p:
            i_sends[p - 1].wait_recv()
        _, in_0, in_1, in_2 = which(p)
        inf = ifb[p].astype(jnp.float32)
        b0, b1, b2 = (
            jnp.where(jnp.broadcast_to(m[:1], inf.shape), inf, 0.0).astype(jnp.bfloat16) for m in (in_0, in_1, in_2)
        )
        g = dot_nt(amask[p], jnp.concatenate([b0, b1, b1, b0, b2, b2], axis=0))
        g = g.reshape(rank // 2, 16, 3 * width)
        even, odd = g[:, :8, :], g[:, 8:, :]
        g0 = jnp.where(low, even[:, :, :width], odd[:, :, width:2 * width])
        g1 = jnp.where(low, even[:, :, width:2 * width], odd[:, :, :width])
        g2 = jnp.where(low, even[:, :, 2 * width:], odd[:, :, 2 * width:])
        gd[p, 0] = g0
        gd[p, 1] = g1
        gd[p, 2] = g2

    for copy in q_sends:
        copy.wait_recv()
    queries = qall[...].reshape(nd * 2 * rows_q, half)
    pairs = rank // 4
    total = []
    at_slot = [lax.rem(qi + nq - j, nq) for j in range(nq)]
    spare = sbuf.shape[2] - nq * DOC_DEV - 8
    for h in range(2):
        part = pl.ds(h * pairs, pairs)
        blocks = []
        for j in range(nq):
            first = gd[at_slot[j], 0, part]
            if j:
                first = first + gd[at_slot[j - 1], 2, part]
            blocks += [first, gd[at_slot[j], 1, part]]
        blocks += [gd[at_slot[nq - 1], 2, part], jnp.zeros((pairs, spare, width), jnp.float32)]
        blocks = jnp.concatenate(blocks, axis=1).astype(jnp.bfloat16)
        docs = jnp.concatenate([blocks[m] for m in range(pairs)], axis=1)
        total.append(dot_nt(queries, docs))
    for p in range(nd):
        at = 2 * p * rows_q
        sbuf[p] = total[0][at:at + rows_q] + total[1][at + rows_q:at + 2 * rows_q]
    s_sends = [remote(sbuf.at[p], rbuf.at[p], ss.at[p], sr.at[p], dp_peer(nd - p)) for p in range(1, nd)]
    for copy in s_sends:
        copy.start()
    rbuf[0] = sbuf[0]
    for copy in s_sends:
        copy.wait_recv()

    per_row = nq * DOC_DEV
    got = [rbuf[lax.rem(r + nd - di, nd)] for r in range(nd)]
    if per_row % 128 == 0:
        for r in range(nd):
            value = got[r][:, :per_row]
            if r:
                value = value + jnp.pad(got[r - 1][:, per_row:per_row + 128], ((0, 0), (0, per_row - 128)))
            out[:, r * per_row:(r + 1) * per_row] = value
    else:
        left = lax.broadcasted_iota(jnp.int32, got[0].shape, 1) < 64
        turned = [pltpu.roll(got[r], 64, 1) if r % 2 else None for r in range(nd)]
        for m in range(nd // 2):
            value = got[2 * m] + jnp.where(left, 0.0, turned[2 * m + 1])
            if m:
                value = value + jnp.where(left, turned[2 * m - 1], 0.0)
            out[:, m * 128:(m + 1) * 128] = value
    for copy in q_sends + o_sends + i_sends + s_sends:
        copy.wait_send()


def solution(mesh):
    nd, nq = mesh.shape["dp"], mesh.shape["query"]

    def on_device(hidden, out_grad, doc_ids, proj_in, proj_out, query_grads):
        tok, ff = hidden.shape
        d = out_grad.shape[1]
        rank = proj_in.shape[0]
        rows_q, flat = query_grads.shape
        per_row = nq * DOC_DEV
        assert rank == 64 and flat == rank * rank and (per_row == 64 or per_row % 128 == 0)
        docs = -(-(per_row + 16) // 128) * 128
        bf16, f32 = jnp.bfloat16, jnp.float32
        dma = pltpu.SemaphoreType.DMA
        hbm = pl.BlockSpec(memory_space=pltpu.HBM)
        vmem = pl.BlockSpec(memory_space=pltpu.VMEM)
        return pl.pallas_call(
            functools.partial(kernel, nd, nq),
            out_shape=jax.ShapeDtypeStruct((rows_q, nd * per_row), f32),
            in_specs=[hbm] * 6,
            out_specs=vmem,
            scratch_shapes=[
                pltpu.VMEM((tok, ff), bf16),
                pltpu.VMEM((tok, d), bf16),
                pltpu.VMEM((rank, ff), bf16),
                pltpu.VMEM((rank, d), bf16),
                pltpu.VMEM((1, tok), jnp.int32),
                pltpu.VMEM((rows_q, flat), bf16),
                pltpu.VMEM((nd, 2 * rows_q, flat // 2), bf16),
                pltpu.VMEM((nq, rank + 16, tok), bf16),
                pltpu.VMEM((nq, rank, tok), bf16),
                pltpu.VMEM((nq, 8 * rank, tok), bf16),
                pltpu.VMEM((nq, 3, rank // 2, 8, 2 * rank), f32),
                pltpu.VMEM((nd, rows_q, docs), f32),
                pltpu.VMEM((nd, rows_q, docs), f32),
                dma((len(H_WIDTHS),)),
                dma((len(O_WIDTHS),)),
                dma((len(H_WIDTHS),)),
                dma((len(O_WIDTHS),)),
                dma((2,)),
                dma((nd,)),
                dma((nd,)),
                dma((nq,)),
                dma((nq,)),
                dma((nq,)),
                dma((nq,)),
                dma((nd,)),
                dma((nd,)),
            ],
            compiler_params=pltpu.CompilerParams(
                collective_id=0, has_side_effects=True, vmem_limit_bytes=60 * 1024 * 1024
            ),
        )(hidden, out_grad, doc_ids.reshape(1, tok), proj_in, proj_out, query_grads)

    placed = (
        P(("groups", "dp", "query"), None),
        P(("groups", "dp", "query"), None),
        P(("groups", "dp", "query")),
        P(),
        P(),
        P(("dp", "query"), None),
    )
    return jax.shard_map(
        on_device, mesh=mesh, in_specs=placed, out_specs=P(("dp", "query"), "groups"), check_vma=False
    )
```
